32 devices in a mesh: ens: 2 (over x), lat: 16 (over z, y, core).
Axes of the slice: x: 2, y: 2, z: 4, core: 2. Of those that a mesh axis runs over, the one named last changes fastest.
Arguments:
- state_field: bfloat16 [64, 768, 320], P(('ens', 'lat')), parts along dimension 0, may hold values from -6 to 6
- noise_field: bfloat16 [64, 768, 320], P(('ens', 'lat')), parts along dimension 0, may hold values from -6 to 6
- noise_scale: float32 [320], replicated, may hold values from 0.1 to 1
- basis_filter: float32 [3, 32, 3, 3], replicated, may hold values from -1 to 1
- row_index: int32 [32, 3], replicated, may hold values from 0 to 31, as said below
- basis_weight: float32 [3, 320], replicated, may hold values from -2 to 2
- spectral_gain: float32 [80, 320], replicated, may hold values from -1.5 to 1.5
- cotangent: bfloat16 [64, 768, 320], P(('ens', 'lat')), parts along dimension 0, may hold values from -18 to 18
Outputs:
- field_grad: bfloat16 [64, 768, 320], P(('ens', 'lat')), parts along dimension 0
- basis_grad: float32 [6, 320], P('ens'), parts along dimension 0
- gain_grad: float32 [160, 320], P('ens'), parts along dimension 0
- scale_grad: float32 [640], P('ens'), parts along dimension 0
The draws below stay inside these ranges and needn't reach their ends.
There are 2 independent parts, one for each index of `ens`. The reference program is written for one: setup_inputs(seed, part) draws one part's arguments, and reference() takes and returns one part's arrays. A program takes and returns all parts, laid end to end along the dimension named above; an argument that names none is the same for every part. Nothing has to cross between parts.
Inputs may be any that keep to these rules, and one draw needn't show every extreme that they name: row_index[i, 1] = i; row_index[i, 0] lies in i - 2 to i - 1 and row_index[i, 2] in i + 1 to i + 2, each clipped to the grid.
All inputs are finite; a program needn't handle non-finite values.
Results may differ from the reference program's by a relative error of at most 0.0091.
Values may be sent and summed in bfloat16 or wider, within the bound.
A program may use at most 128 MiB of HBM per device.

```python
import math
import jax
import jax.numpy as jnp
from jax import lax

C = 320
NLON = 768
LAT_DEV = 2
TAPS = 3
BASIS = 3
NLAT = 32
MMAX = 80
LMAX = 80


def draw_row_index(key, part):
    key = jax.random.fold_in(key, 11)
    up_key, down_key = jax.random.split(key)
    centre = jnp.arange(NLAT, dtype=jnp.int32)
    above_rows = centre - jax.random.randint(up_key, (NLAT,), 1, LAT_DEV + 1, dtype=jnp.int32)
    below_rows = centre + jax.random.randint(down_key, (NLAT,), 1, LAT_DEV + 1, dtype=jnp.int32)
    return jnp.stack([jnp.clip(above_rows, 0, NLAT - 1), centre, jnp.clip(below_rows, 0, NLAT - 1)], axis=1)


def draw_cotangent(key, part):
    key = jax.random.fold_in(key, 23)
    lat_scale = 1.0 + 2.0 * jnp.arange(NLAT, dtype=jnp.float32) / (NLAT - 1)
    raw_values = jnp.clip(jax.random.normal(key, (NLAT, NLON, C), jnp.float32), -6.0, 6.0)
    return (raw_values * lat_scale[:, None, None]).astype(jnp.bfloat16)


def block_scale(rng, dims, shards, low, largest):
    factor_of = 1.0
    for axis_at, parts in shards:
        heights = jax.random.uniform(jax.random.fold_in(jax.random.fold_in(rng, 6), axis_at), (parts,), jnp.float32, low / len(shards), largest / len(shards))
        factor_of = factor_of * jnp.repeat(jnp.exp(heights), dims[axis_at] // parts).reshape((-1,) + (1,) * (len(dims) - 1 - axis_at))
    return factor_of


def normal_values(key, extent, deviation, reach, pieces=(), held_as=jnp.bfloat16):
    array = deviation * jax.random.normal(key, extent, jnp.float32)
    if pieces:
        array = array * block_scale(key, extent, pieces, -0.22, 0.18)
    return jnp.clip(array, -reach, reach).astype(held_as)


def setup_inputs(seed: int = 0, part: int = 0) -> dict:
    arg_keys = jax.random.split(jax.random.key(seed), 9)
    part_keys = jax.random.split(jax.random.fold_in(arg_keys[8], part), 9)
    state_field = normal_values(part_keys[0], (NLAT, NLON, C), 1.0, 6.0, ((0, 16),))
    noise_field = normal_values(part_keys[1], (NLAT, NLON, C), 1.0, 6.0, ((0, 16),))
    noise_scale = jnp.clip(jnp.exp(jax.random.uniform(arg_keys[2], (C,), jnp.float32, math.log(0.1), math.log(1.0))), 0.1, 1.0)
    basis_filter = jnp.clip(jax.random.uniform(arg_keys[3], (BASIS, NLAT, TAPS, 3), jnp.float32, -1.0, 1.0), -1.0, 1.0)
    row_index = draw_row_index(jax.random.fold_in(arg_keys[8], 71), part)
    basis_weight = normal_values(arg_keys[5], (BASIS, C), 0.33, 2.0, (), jnp.float32)
    spectral_gain = jnp.clip(jax.random.uniform(arg_keys[6], (LMAX, C), jnp.float32, -1.5, 1.5), -1.5, 1.5)
    cotangent = draw_cotangent(jax.random.fold_in(jax.random.fold_in(arg_keys[8], part), 71), part)
    return dict(state_field=state_field, noise_field=noise_field, noise_scale=noise_scale, basis_filter=basis_filter, row_index=row_index, basis_weight=basis_weight, spectral_gain=spectral_gain, cotangent=cotangent)


def legendre_table(orders_used, lat_count, degree_count):
    row_float = jnp.arange(lat_count, dtype=jnp.float32)
    colatitude = jnp.pi * (row_float + 0.5) / lat_count
    cos_lat = jnp.cos(colatitude)
    sine_lat = jnp.sin(colatitude)
    counter = jnp.arange(1, degree_count + 1, dtype=jnp.float32)
    log_terms = 0.5 * jnp.log((2.0 * counter + 1.0) / (2.0 * counter))
    partial_sum = lax.optimization_barrier(jnp.sum(jnp.where(counter[None, :] <= orders_used[:, None], log_terms[None, :], 0.0), axis=1))
    log_start = 0.5 * jnp.log(1.0 / (4.0 * jnp.pi)) + partial_sum[:, None] + orders_used[:, None] * jnp.log(sine_lat)[None, :]
    diagonal_start = jnp.exp(log_start)
    order_col = orders_used[:, None]

    def advance(carried, degree):
        prev_one, prev_two = carried
        degree_float = degree.astype(jnp.float32)
        ratio_a = jnp.sqrt((4.0 * degree_float * degree_float - 1.0) / jnp.maximum(degree_float * degree_float - order_col * order_col, 1.0))
        ratio_b = jnp.sqrt(jnp.maximum((degree_float - 1.0) ** 2 - order_col * order_col, 0.0) / jnp.maximum(4.0 * (degree_float - 1.0) ** 2 - 1.0, 1.0))
        general = ratio_a * (cos_lat[None, :] * prev_one - ratio_b * prev_two)
        current = jnp.where(degree_float < order_col, 0.0, jnp.where(degree_float == order_col, diagonal_start, general))
        return ((current, prev_one), current)
    blank_rows = jnp.zeros((orders_used.shape[0], lat_count), jnp.float32)
    _, stacked = lax.scan(advance, (blank_rows, blank_rows), jnp.arange(degree_count, dtype=jnp.int32), unroll=16)
    return jnp.transpose(stacked, (1, 0, 2))

def quadrature(lat_count):
    row_float = jnp.arange(lat_count, dtype=jnp.float32)
    return jnp.pi / lat_count * jnp.sin(jnp.pi * (row_float + 0.5) / lat_count)

def transform_tables(lon_count, mode_count):
    points = jnp.arange(lon_count, dtype=jnp.int32)
    orders = jnp.arange(mode_count, dtype=jnp.int32)
    phases = (points[:, None] * orders[None, :] % lon_count).astype(jnp.float32) * (2.0 * jnp.pi / lon_count)
    forward = jnp.stack([jnp.cos(phases), -jnp.sin(phases)], axis=-1) * (2.0 * jnp.pi / lon_count)
    weight_m = jnp.where(orders == 0, 1.0, 2.0).astype(jnp.float32)
    inverse = jnp.stack([jnp.cos(phases), -jnp.sin(phases)], axis=-1) * weight_m[None, :, None]
    return (forward.astype(jnp.bfloat16), jnp.transpose(inverse, (1, 2, 0)).astype(jnp.bfloat16))

def gelu_tanh(pre_act):
    return jax.nn.gelu(pre_act, approximate=True)

def reference(state_field, noise_field, noise_scale, basis_filter, row_index, basis_weight, spectral_gain, cotangent):
    highest = lax.Precision.HIGHEST
    start_field = (state_field.astype(jnp.float32) + noise_scale * noise_field.astype(jnp.float32)).astype(jnp.bfloat16)
    coeffs = jnp.einsum('kits,kc->itsc', basis_filter, basis_weight, precision=highest)
    local_sum = jnp.zeros(start_field.shape, jnp.float32)
    for tap_no in range(TAPS):
        picked = start_field[row_index[:, tap_no]].astype(jnp.float32)
        for offset in range(3):
            local_sum = local_sum + coeffs[:, tap_no, offset, None, :] * jnp.roll(picked, 1 - offset, axis=1)
    forward, inverse = transform_tables(NLON, MMAX)
    legendre = legendre_table(jnp.arange(MMAX, dtype=jnp.float32), NLAT, LMAX)
    analysis = (legendre * quadrature(NLAT)[None, None, :]).astype(jnp.bfloat16).astype(jnp.float32)
    synthesis = legendre.astype(jnp.bfloat16).astype(jnp.float32)
    forward_wide = forward.astype(jnp.float32)
    inverse_wide = inverse.astype(jnp.float32)
    spectra = jnp.einsum('jnc,nmr->jmrc', start_field.astype(jnp.float32), forward_wide).astype(jnp.bfloat16)
    coefficients = jnp.einsum('mlj,jmrc->mlrc', analysis, spectra.astype(jnp.float32))
    filtered = (spectral_gain[None, :, None, :] * coefficients).astype(jnp.bfloat16)
    returned = jnp.einsum('mlj,mlrc->jmrc', synthesis, filtered.astype(jnp.float32)).astype(jnp.bfloat16)
    spectral_part = jnp.einsum('jmrc,mrn->jnc', returned.astype(jnp.float32), inverse_wide)
    pre = local_sum + spectral_part
    _, pullback = jax.vjp(gelu_tanh, pre)
    grad_pre = pullback(cotangent.astype(jnp.float32))[0].astype(jnp.bfloat16)
    grad_wide = grad_pre.astype(jnp.float32)
    grad_returned = jnp.einsum('jnc,mrn->jmrc', grad_wide, inverse_wide).astype(jnp.bfloat16)
    grad_coeff = jnp.einsum('mlj,jmrc->mlrc', synthesis, grad_returned.astype(jnp.float32))
    gain_grad = lax.optimization_barrier(jnp.sum(coefficients * grad_coeff, axis=(0, 2)))
    grad_filtered = (spectral_gain[None, :, None, :] * grad_coeff).astype(jnp.bfloat16)
    grad_spectra = jnp.einsum('mlj,mlrc->jmrc', analysis, grad_filtered.astype(jnp.float32)).astype(jnp.bfloat16)
    spectral_back = jnp.einsum('jmrc,nmr->jnc', grad_spectra.astype(jnp.float32), forward_wide)
    local_back = jnp.zeros(start_field.shape, jnp.float32)
    products = []
    for tap_no in range(TAPS):
        picked = start_field[row_index[:, tap_no]].astype(jnp.float32)
        spread = jnp.zeros(start_field.shape, jnp.float32)
        tap_products = []
        for offset in range(3):
            spread = spread + coeffs[:, tap_no, offset, None, :] * jnp.roll(grad_wide, offset - 1, axis=1)
            tap_products.append(lax.optimization_barrier(jnp.sum(grad_wide * jnp.roll(picked, 1 - offset, axis=1), axis=1)))
        products.append(jnp.stack(tap_products, axis=1))
        local_back = local_back.at[row_index[:, tap_no]].add(spread)
    products = jnp.stack(products, axis=1)
    basis_grad = jnp.einsum('kits,itsc->kc', basis_filter, products, precision=highest)
    grad_sum = spectral_back + local_back
    scale_grad = lax.optimization_barrier(jnp.sum(grad_sum * noise_field.astype(jnp.float32), axis=(0, 1)))
    return (grad_sum.astype(jnp.bfloat16), basis_grad, gain_grad, scale_grad)
```

```python
import functools
import math

import jax
import jax.numpy as jnp
import numpy as np
from jax import lax
from jax.experimental import pallas as pl
from jax.experimental.pallas import tpu as pltpu
from jax.sharding import PartitionSpec as P

F32, BF16 = jnp.float32, jnp.bfloat16
MESH = pl.DeviceIdType.MESH
SLOTS = 16


def legendre_numpy(modes, lats, degrees):
    u = np.pi * (np.arange(lats) + 0.5) / lats
    order = np.arange(modes, dtype=np.float64)[:, None]
    k = np.arange(1, modes + 1, dtype=np.float64)
    steps = np.concatenate([[0.0], np.cumsum(0.5 * np.log((2 * k + 1) / (2 * k)))])[:modes]
    start = np.exp(
        0.5 * np.log(1 / (4 * np.pi)) + steps[:, None] + order * np.log(np.sin(u))[None, :]
    )
    out = np.zeros((modes, degrees, lats))
    one = np.zeros((modes, lats))
    two = np.zeros((modes, lats))
    for l in range(degrees):
        a = np.sqrt((4.0 * l * l - 1 if l else 0.0) / np.maximum(l * l - order**2, 1.0))
        b = np.sqrt(
            np.maximum((l - 1.0) ** 2 - order**2, 0.0) / np.maximum(4 * (l - 1.0) ** 2 - 1, 1.0)
        )
        general = a * (np.cos(u)[None, :] * one - b * two)
        now = np.where(l < order, 0.0, np.where(l == order, start, general))
        out[:, l] = now
        one, two = now, one
    weight = np.pi / lats * np.sin(u)
    return (out * weight).astype(jnp.bfloat16), out.astype(jnp.bfloat16)


def fourier_numpy(lons, devices, each):
    modes = devices * each
    n = np.arange(lons)
    m = np.arange(modes)
    p = 2 * np.pi * ((n[None, :] * m[:, None]) % lons) / lons
    pair = np.stack([np.cos(p), -np.sin(p)], axis=1)
    forward = pair * (2 * np.pi / lons)
    inverse = pair * np.where(m == 0, 1.0, 2.0)[:, None, None]

    def padded(table):
        out = np.zeros((devices, SLOTS, lons))
        out[:, : 2 * each] = table.reshape(devices, 2 * each, lons)
        return out.reshape(devices * SLOTS, lons).astype(jnp.bfloat16)

    return padded(forward), padded(inverse)


def dot(a, b):
    return lax.dot_general(a, b, (((1,), (0,)), ((), ())), preferred_element_type=F32)


def dot_turned(a, b):
    return lax.dot_general(a, b, (((0,), (0,)), ((), ())), preferred_element_type=F32)


def kernel(
    dims,
    filt,
    rows,
    state,
    noise,
    cot,
    scale,
    weight,
    gain,
    fwd,
    fwd_t,
    inv,
    inv_t,
    pick,
    pick_t,
    table,
    out,
    basis_out,
    gain_out,
    scale_out,
    pad,
    gpad,
    ls,
    ysc,
    cf,
    ef,
    coef,
    gacc,
    pencil,
    sorted_rows,
    send,
    recv,
    gain_in,
    gain_sum,
    small,
    small_in,
    a2a_send,
    a2a_recv,
    halo_send,
    halo_recv,
    gain_send,
    gain_recv,
    gat_send,
    gat_recv,
    small_send,
    small_recv,
):
    devices, each, lons, chans, degrees, lats = dims
    span = 2
    me = lax.axis_index("lat")
    first = me * span
    chunk, wide = 32, 128
    groups = chunk // 8
    reducers = degrees // 8

    def peer_of(off):
        return lax.rem(me + off, devices)

    def source_of(off):
        return lax.rem(me - off + devices, devices)

    barrier = pltpu.get_barrier_semaphore()

    def greet(off, z):
        pl.semaphore_signal(barrier, inc=1, device_id={"lat": peer_of(off)}, device_id_type=MESH)
        return z

    lax.fori_loop(1, devices, greet, 0)

    def block_copy(phase, off, peer):
        return pltpu.make_async_remote_copy(
            src_ref=send.at[phase, peer],
            dst_ref=recv.at[phase, me],
            send_sem=a2a_send.at[phase, off],
            recv_sem=a2a_recv.at[phase, off],
            device_id={"lat": peer},
            device_id_type=MESH,
        )

    def exchange(phase):
        def go(off, z):
            block_copy(phase, off, peer_of(off)).start()
            return z

        lax.fori_loop(1, devices, go, 0)
        recv[phase, me] = send[phase, me]

    def arrive(phase):
        def take(off, z):
            block_copy(phase, off, peer_of(off)).wait_recv()
            return z

        lax.fori_loop(1, devices, take, 0)

    def halo_copies(buffer, phase):
        up = pltpu.make_async_remote_copy(
            src_ref=buffer.at[pl.ds(2, 2)],
            dst_ref=buffer.at[pl.ds(4, 2)],
            send_sem=halo_send.at[phase, 0],
            recv_sem=halo_recv.at[phase, 0],
            device_id={"lat": lax.rem(me + devices - 1, devices)},
            device_id_type=MESH,
        )
        down = pltpu.make_async_remote_copy(
            src_ref=buffer.at[pl.ds(2, 2)],
            dst_ref=buffer.at[pl.ds(0, 2)],
            send_sem=halo_send.at[phase, 1],
            recv_sem=halo_recv.at[phase, 1],
            device_id={"lat": lax.rem(me + 1, devices)},
            device_id_type=MESH,
        )
        return up, down

    def halo_start(buffer, phase):
        up, down = halo_copies(buffer, phase)

        @pl.when(me > 0)
        def _():
            up.start()

        @pl.when(me < devices - 1)
        def _():
            down.start()

    def halo_arrive(buffer, phase):
        up, down = halo_copies(buffer, phase)

        @pl.when(me < devices - 1)
        def _():
            up.wait_recv()

        @pl.when(me > 0)
        def _():
            down.wait_recv()

    def halo_sent(buffer, phase):
        up, down = halo_copies(buffer, phase)

        @pl.when(me > 0)
        def _():
            up.wait_send()

        @pl.when(me < devices - 1)
        def _():
            down.wait_send()

    def at(c, size=chunk):
        return pl.ds(pl.multiple_of(c * size, size), size)

    def around(c, shift):
        return pl.ds(pl.multiple_of(c * chunk + shift, 8), chunk + 8)

    def before(x):
        return pltpu.roll(x, 1, 0)[8:]

    def after(x):
        return pltpu.roll(x, chunk + 7, 0)[:chunk]

    def tall(x):
        return x.reshape(groups, 8, chans)

    sc = scale[...]
    for j in range(span):

        def noisy(c, z):
            pad[2 + j, at(c)] = (
                state[j, at(c)].astype(F32) + sc * noise[j, at(c)].astype(F32)
            ).astype(BF16)
            return z

        lax.fori_loop(0, lons // chunk, noisy, 0)
        send[0, :, j] = (
            dot(fwd[...], pad[2 + j]).astype(BF16).reshape(devices, SLOTS, chans)
        )

    pl.semaphore_wait(barrier, devices - 1)
    exchange(0)
    halo_start(pad, 0)

    @pl.when(me == 0)
    def _():
        pad[0:2] = jnp.zeros((2, lons, chans), BF16)
        gpad[0:2] = jnp.zeros((2, lons, chans), BF16)

    @pl.when(me == devices - 1)
    def _():
        pad[4:6] = jnp.zeros((2, lons, chans), BF16)
        gpad[4:6] = jnp.zeros((2, lons, chans), BF16)

    def filter_row(row, t, s):
        total = jnp.zeros((1, chans), F32)
        for k in range(3):
            total = total + filt[((k * lats + row) * 3 + t) * 3 + s] * weight[k : k + 1, :]
        return total

    for i in range(span):
        for t in range(3):
            for s in range(3):
                cf[i * 9 + t * 3 + s] = jnp.broadcast_to(
                    filter_row(first + i, t, s), (8, chans)
                )
    for q in range(span):
        for e in range(5):
            row = lax.rem(first - 2 + q + e + lats, lats)
            taps = (2,) if e < 2 else ((0,) if e > 2 else (0, 1, 2))
            for s in range(3):
                total = jnp.zeros((1, chans), F32)
                for t in taps:
                    hit = jnp.where(rows[row * 3 + t] == first + q, 1.0, 0.0).astype(F32)
                    total = total + hit * filter_row(row, t, s)
                ef[q * 15 + e * 3 + s] = jnp.broadcast_to(total, (8, chans))

    arrive(0)

    def gather_rows(phase):
        block = recv[phase].reshape(devices * span * SLOTS, chans)
        pieces = max(devices // 16, 1)
        size = 2 * each * lats // pieces
        for piece in range(pieces):
            part = pl.ds(piece * size, size)
            pencil[part] = dot(pick[part], block).astype(BF16)

    def scatter_rows(phase):
        pieces = max(devices // 16, 1)
        size = devices // pieces
        for piece in range(pieces):
            part = pl.ds(piece * size * span * SLOTS, size * span * SLOTS)
            send[phase, pl.ds(piece * size, size)] = (
                dot(pick_t[part], sorted_rows[...]).astype(BF16).reshape(size, span, SLOTS, chans)
            )

    gather_rows(0)
    gains = gain[...]

    def analyse(m, z):
        for r in range(2):
            cm = dot(table[0, at(m, degrees)], pencil[at(2 * m + r, lats)])
            coef[2 * m + r] = cm
            sorted_rows[at(2 * m + r, lats)] = dot_turned(
                table[1, at(m, degrees)], (gains * cm).astype(BF16)
            ).astype(BF16)
        return z

    lax.fori_loop(0, each, analyse, 0)
    scatter_rows(1)
    exchange(1)

    halo_arrive(pad, 0)

    def picked(i, t, c):
        slot = jnp.clip(rows[(first + i) * 3 + t] - first + 2, 0, 5)
        return pad[slot, at(c)].astype(F32)

    for i in range(span):

        def taps_of(c, z):
            y = [None, None, None]
            for t in range(3):
                x = tall(picked(i, t, c))
                for s in range(3):
                    term = cf[i * 9 + t * 3 + s][None] * x
                    y[s] = term if t == 0 else y[s] + term
            here = pl.ds(pl.multiple_of(8 + c * chunk, 8), chunk)
            ysc[0, here] = y[0].reshape(chunk, chans)
            ysc[1, here] = y[2].reshape(chunk, chans)
            ls[i, at(c)] = y[1].reshape(chunk, chans)
            return z

        lax.fori_loop(0, lons // chunk, taps_of, 0)
        ysc[0, 7:8] = ysc[0, lons + 7 : lons + 8]
        ysc[1, lons + 8 : lons + 9] = ysc[1, 8:9]

        def join(c, z):
            ls[i, at(c)] += (
                before(ysc[0, around(c, 0)]) + after(ysc[1, around(c, 8)])
            )
            return z

        lax.fori_loop(0, lons // chunk, join, 0)

    arrive(1)

    root = math.sqrt(2.0 / math.pi)
    for j in range(span):
        returned = recv[1, :, j].reshape(devices * SLOTS, chans)

        def activate(c, z):
            v = ls[j, at(c, wide)] + dot(inv_t[at(c, wide)], returned)
            square = v * v
            th = jnp.tanh(root * v * (1.0 + 0.044715 * square))
            slope = 0.5 * (1.0 + th) + 0.5 * v * (1.0 - th * th) * root * (
                1.0 + 3 * 0.044715 * square
            )
            gpad[2 + j, at(c, wide)] = (cot[j, at(c, wide)].astype(F32) * slope).astype(BF16)
            return z

        lax.fori_loop(0, lons // wide, activate, 0)
        send[2, :, j] = (
            dot(inv[...], gpad[2 + j]).astype(BF16).reshape(devices, SLOTS, chans)
        )
    exchange(2)
    halo_start(gpad, 1)

    basis = [jnp.zeros((1, chans), F32) for _ in range(3)]
    for i in range(span):

        def widen(c, z):
            ysc[0, pl.ds(pl.multiple_of(8 + c * chunk, 8), chunk)] = gpad[2 + i, at(c)].astype(F32)
            return z

        lax.fori_loop(0, lons // chunk, widen, 0)
        ysc[0, 7:8] = ysc[0, lons + 7 : lons + 8]
        ysc[0, lons + 8 : lons + 9] = ysc[0, 8:9]

        def correlate(c, sums):
            g = [
                tall(after(ysc[0, around(c, 8)])),
                tall(ysc[0, pl.ds(pl.multiple_of(8 + c * chunk, 8), chunk)]),
                tall(before(ysc[0, around(c, 0)])),
            ]
            new = []
            for t in range(3):
                x = tall(picked(i, t, c))
                for s in range(3):
                    new.append(sums[t * 3 + s] + jnp.sum(g[s] * x, axis=0))
            return tuple(new)

        sums = lax.fori_loop(
            0, lons // chunk, correlate, tuple(jnp.zeros((8, chans), F32) for _ in range(9))
        )
        for t in range(3):
            for s in range(3):
                total = jnp.sum(sums[t * 3 + s], axis=0, keepdims=True)
                for k in range(3):
                    basis[k] = (
                        basis[k] + filt[((k * lats + first + i) * 3 + t) * 3 + s] * total
                    )
    small[...] = jnp.zeros((8, chans), F32)
    for k in range(3):
        small[k : k + 1] = basis[k]

    arrive(2)
    gather_rows(2)
    gacc[...] = jnp.zeros((degrees, chans), F32)

    def analyse_back(m, z):
        for r in range(2):
            gm = dot(table[1, at(m, degrees)], pencil[at(2 * m + r, lats)])
            gacc[...] += coef[2 * m + r] * gm
            sorted_rows[at(2 * m + r, lats)] = dot_turned(
                table[0, at(m, degrees)], (gains * gm).astype(BF16)
            ).astype(BF16)
        return z

    lax.fori_loop(0, each, analyse_back, 0)
    scatter_rows(3)
    exchange(3)

    def gain_copy(off, peer):
        return pltpu.make_async_remote_copy(
            src_ref=gacc.at[pl.ds(pl.multiple_of(lax.rem(peer, reducers) * 8, 8), 8)],
            dst_ref=gain_in.at[me],
            send_sem=gain_send.at[off],
            recv_sem=gain_recv.at[off],
            device_id={"lat": peer},
            device_id_type=MESH,
        )

    def total_copy(off, peer):
        return pltpu.make_async_remote_copy(
            src_ref=gain_sum.at[me],
            dst_ref=gain_sum.at[me],
            send_sem=gat_send.at[off],
            recv_sem=gat_recv.at[off],
            device_id={"lat": peer},
            device_id_type=MESH,
        )

    def gain_go(off, z):
        peer = peer_of(off)

        @pl.when(peer < reducers)
        def _():
            gain_copy(off, peer).start()

        return z

    lax.fori_loop(1, devices, gain_go, 0)

    halo_arrive(gpad, 1)
    for q in range(span):

        def spread_of(c, z):
            y = [None, None, None]
            for e in range(5):
                x = tall(gpad[q + e, at(c)].astype(F32))
                for s in range(3):
                    term = ef[q * 15 + e * 3 + s][None] * x
                    y[s] = term if e == 0 else y[s] + term
            here = pl.ds(pl.multiple_of(8 + c * chunk, 8), chunk)
            ysc[0, here] = y[2].reshape(chunk, chans)
            ysc[1, here] = y[0].reshape(chunk, chans)
            ls[q, at(c)] = y[1].reshape(chunk, chans)
            return z

        lax.fori_loop(0, lons // chunk, spread_of, 0)
        ysc[0, 7:8] = ysc[0, lons + 7 : lons + 8]
        ysc[1, lons + 8 : lons + 9] = ysc[1, 8:9]

        def join_back(c, z):
            ls[q, at(c)] += (
                before(ysc[0, around(c, 0)]) + after(ysc[1, around(c, 8)])
            )
            return z

        lax.fori_loop(0, lons // chunk, join_back, 0)

    @pl.when(me < reducers)
    def _():
        gain_in[me] = gacc[pl.ds(pl.multiple_of(lax.rem(me, reducers) * 8, 8), 8)]

        def take(off, z):
            gain_copy(off, peer_of(off)).wait_recv()
            return z

        lax.fori_loop(1, devices, take, 0)
        gain_sum[me] = jnp.sum(gain_in[...], axis=0)

        def give(off, z):
            total_copy(off, peer_of(off)).start()
            return z

        lax.fori_loop(1, devices, give, 0)

    arrive(3)
    accs = jnp.zeros((8, chans), F32)
    for j in range(span):
        back = recv[3, :, j].reshape(devices * SLOTS, chans)

        def finish(c, acc):
            total = ls[j, at(c, wide)] + dot(fwd_t[at(c, wide)], back)
            out[j, at(c, wide)] = total.astype(BF16)
            prod = total * noise[j, at(c, wide)].astype(F32)
            return acc + jnp.sum(prod.reshape(wide // 8, 8, chans), axis=0)

        accs = lax.fori_loop(0, lons // wide, finish, accs)
    small[3:4] = jnp.sum(accs, axis=0, keepdims=True)

    def small_copy(off, peer):
        return pltpu.make_async_remote_copy(
            src_ref=small,
            dst_ref=small_in.at[me],
            send_sem=small_send.at[off],
            recv_sem=small_recv.at[off],
            device_id={"lat": peer},
            device_id_type=MESH,
        )

    def small_go(off, z):
        small_copy(off, peer_of(off)).start()
        return z

    lax.fori_loop(1, devices, small_go, 0)
    small_in[me] = small[...]

    def gain_take(off, z):
        @pl.when(source_of(off) < reducers)
        def _():
            total_copy(off, peer_of(off)).wait_recv()

        return z

    lax.fori_loop(1, devices, gain_take, 0)
    gain_out[...] = gain_sum[0:reducers].reshape(degrees, chans)

    def small_take(off, z):
        small_copy(off, peer_of(off)).wait_recv()
        return z

    lax.fori_loop(1, devices, small_take, 0)
    sums = jnp.sum(small_in[...], axis=0)
    basis_out[...] = sums[0:3]
    scale_out[...] = sums[3:4]

    def sent(off, z):
        peer = peer_of(off)
        for phase in range(4):
            block_copy(phase, off, peer).wait_send()
        small_copy(off, peer).wait_send()

        @pl.when(peer < reducers)
        def _():
            gain_copy(off, peer).wait_send()

        @pl.when(me < reducers)
        def _():
            total_copy(off, peer).wait_send()

        return z

    lax.fori_loop(1, devices, sent, 0)
    halo_sent(pad, 0)
    halo_sent(gpad, 1)


def body(state, noise, scale, filt, rows, weight, gain, cot):
    devices = lax.axis_size("lat")
    span, lons, chans = state.shape
    degrees = gain.shape[0]
    lats = span * devices
    each = degrees // devices
    analysis, synthesis = legendre_numpy(degrees, lats, degrees)
    forward, inverse = fourier_numpy(lons, devices, each)

    tables = np.stack(
        [t.reshape(devices, each * degrees, lats) for t in (analysis, synthesis)], axis=1
    )
    table = lax.dynamic_index_in_dim(tables, lax.axis_index("lat"), 0, keepdims=False)
    pick = np.zeros((2 * each, lats, lats, SLOTS), jnp.bfloat16)
    for slot in range(2 * each):
        pick[slot, np.arange(lats), np.arange(lats), slot] = 1
    pick = pick.reshape(2 * each * lats, lats * SLOTS)
    vmem = pl.BlockSpec(memory_space=pltpu.VMEM)
    smem = pl.BlockSpec(memory_space=pltpu.SMEM)
    dma = pltpu.SemaphoreType.DMA
    out, basis, gains, scales = pl.pallas_call(
        functools.partial(kernel, (devices, each, lons, chans, degrees, lats)),
        out_shape=(
            jax.ShapeDtypeStruct((span, lons, chans), BF16),
            jax.ShapeDtypeStruct((3, chans), F32),
            jax.ShapeDtypeStruct((degrees, chans), F32),
            jax.ShapeDtypeStruct((1, chans), F32),
        ),
        in_specs=[smem, smem] + [vmem] * 13,
        out_specs=(vmem,) * 4,
        scratch_shapes=[
            pltpu.VMEM((6, lons, chans), BF16),
            pltpu.VMEM((6, lons, chans), BF16),
            pltpu.VMEM((2, lons, chans), F32),
            pltpu.VMEM((2, lons + 16, chans), F32),
            pltpu.VMEM((18, 8, chans), F32),
            pltpu.VMEM((30, 8, chans), F32),
            pltpu.VMEM((2 * each, degrees, chans), F32),
            pltpu.VMEM((degrees, chans), F32),
            pltpu.VMEM((2 * each * lats, chans), BF16),
            pltpu.VMEM((2 * each * lats, chans), BF16),
            pltpu.VMEM((4, devices, span, SLOTS, chans), BF16),
            pltpu.VMEM((4, devices, span, SLOTS, chans), BF16),
            pltpu.VMEM((devices, 8, chans), F32),
            pltpu.VMEM((devices, 8, chans), F32),
            pltpu.VMEM((8, chans), F32),
            pltpu.VMEM((devices, 8, chans), F32),
            dma((4, devices)),
            dma((4, devices)),
            dma((2, 2)),
            dma((2, 2)),
            dma((devices,)),
            dma((devices,)),
            dma((devices,)),
            dma((devices,)),
            dma((devices,)),
            dma((devices,)),
        ],
        compiler_params=pltpu.CompilerParams(
            collective_id=0, has_side_effects=True, vmem_limit_bytes=60 * 1024 * 1024
        ),
        name="block_and_gradient",
    )(
        filt.reshape(-1),
        rows.reshape(-1),
        state,
        noise,
        cot,
        scale.reshape(1, chans),
        weight,
        gain,
        forward,
        np.ascontiguousarray(forward.T),
        inverse,
        np.ascontiguousarray(inverse.T),
        pick,
        np.ascontiguousarray(pick.T),
        table,
    )
    return out, basis, gains, scales.reshape(chans)


def solution(mesh):
    field = P(("ens", "lat"), None, None)
    return jax.shard_map(
        body,
        mesh=mesh,
        in_specs=(field, field, P(), P(), P(), P(), P(), field),
        out_specs=(field, P("ens", None), P("ens", None), P("ens")),
        check_vma=False,
    )
```

```python
import functools
import math

import jax
import jax.numpy as jnp
import numpy as np
from jax import lax
from jax.experimental import pallas as pl
from jax.experimental.pallas import tpu as pltpu
from jax.sharding import PartitionSpec as P

F32, BF16 = jnp.float32, jnp.bfloat16
MESH = pl.DeviceIdType.MESH
SLOTS = 16


def legendre_numpy(modes, lats, degrees):
    u = np.pi * (np.arange(lats) + 0.5) / lats
    order = np.arange(modes, dtype=np.float64)[:, None]
    k = np.arange(1, modes + 1, dtype=np.float64)
    steps = np.concatenate([[0.0], np.cumsum(0.5 * np.log((2 * k + 1) / (2 * k)))])[:modes]
    start = np.exp(
        0.5 * np.log(1 / (4 * np.pi)) + steps[:, None] + order * np.log(np.sin(u))[None, :]
    )
    out = np.zeros((modes, degrees, lats))
    one = np.zeros((modes, lats))
    two = np.zeros((modes, lats))
    for l in range(degrees):
        a = np.sqrt((4.0 * l * l - 1 if l else 0.0) / np.maximum(l * l - order**2, 1.0))
        b = np.sqrt(
            np.maximum((l - 1.0) ** 2 - order**2, 0.0) / np.maximum(4 * (l - 1.0) ** 2 - 1, 1.0)
        )
        general = a * (np.cos(u)[None, :] * one - b * two)
        now = np.where(l < order, 0.0, np.where(l == order, start, general))
        out[:, l] = now
        one, two = now, one
    weight = np.pi / lats * np.sin(u)
    return (out * weight).astype(jnp.bfloat16), out.astype(jnp.bfloat16)


def fourier_numpy(lons, devices, each):
    modes = devices * each
    n = np.arange(lons)
    m = np.arange(modes)
    p = 2 * np.pi * ((n[None, :] * m[:, None]) % lons) / lons
    pair = np.stack([np.cos(p), -np.sin(p)], axis=1)
    forward = pair * (2 * np.pi / lons)
    inverse = pair * np.where(m == 0, 1.0, 2.0)[:, None, None]

    def padded(table):
        out = np.zeros((devices, SLOTS, lons))
        out[:, : 2 * each] = table.reshape(devices, 2 * each, lons)
        return out.reshape(devices * SLOTS, lons).astype(jnp.bfloat16)

    return padded(forward), padded(inverse)


def dot(a, b):
    return lax.dot_general(a, b, (((1,), (0,)), ((), ())), preferred_element_type=F32)


def dot_turned(a, b):
    return lax.dot_general(a, b, (((0,), (0,)), ((), ())), preferred_element_type=F32)


def kernel(
    dims,
    filt,
    rows,
    state_far,
    noise_far,
    cot_far,
    scale,
    weight,
    gain,
    fwd,
    fwd_t,
    inv,
    inv_t,
    pick,
    pick_t,
    table,
    out,
    basis_out,
    gain_out,
    scale_out,
    state,
    noise,
    cot,
    field_sem,
    pad,
    gpad,
    ls,
    ysc,
    cf,
    ef,
    coef,
    gacc,
    pencil,
    sorted_rows,
    send,
    recv,
    gain_in,
    gain_sum,
    small,
    small_in,
    a2a_send,
    a2a_recv,
    halo_send,
    halo_recv,
    gain_send,
    gain_recv,
    gat_send,
    gat_recv,
    small_send,
    small_recv,
):
    devices, each, lons, chans, degrees, lats = dims
    span = 2
    me = lax.axis_index("lat")
    first = me * span
    chunk, wide = 32, 128
    groups = chunk // 8
    reducers = degrees // 8

    def peer_of(off):
        return lax.rem(me + off, devices)

    def source_of(off):
        return lax.rem(me - off + devices, devices)

    fields = [
        pltpu.make_async_copy(src, dst, field_sem.at[i])
        for i, (src, dst) in enumerate(((state_far, state), (noise_far, noise), (cot_far, cot)))
    ]
    for copy in fields:
        copy.start()

    barrier = pltpu.get_barrier_semaphore()

    def greet(off, z):
        pl.semaphore_signal(barrier, inc=1, device_id={"lat": peer_of(off)}, device_id_type=MESH)
        return z

    lax.fori_loop(1, devices, greet, 0)

    def block_copy(phase, off, peer):
        return pltpu.make_async_remote_copy(
            src_ref=send.at[phase, peer],
            dst_ref=recv.at[phase, me],
            send_sem=a2a_send.at[phase, off],
            recv_sem=a2a_recv.at[phase, off],
            device_id={"lat": peer},
            device_id_type=MESH,
        )

    def exchange(phase):
        def go(off, z):
            block_copy(phase, off, peer_of(off)).start()
            return z

        lax.fori_loop(1, devices, go, 0)
        recv[phase, me] = send[phase, me]

    def arrive(phase):
        def take(off, z):
            block_copy(phase, off, peer_of(off)).wait_recv()
            return z

        lax.fori_loop(1, devices, take, 0)

    def halo_copies(buffer, phase):
        up = pltpu.make_async_remote_copy(
            src_ref=buffer.at[pl.ds(2, 2)],
            dst_ref=buffer.at[pl.ds(4, 2)],
            send_sem=halo_send.at[phase, 0],
            recv_sem=halo_recv.at[phase, 0],
            device_id={"lat": lax.rem(me + devices - 1, devices)},
            device_id_type=MESH,
        )
        down = pltpu.make_async_remote_copy(
            src_ref=buffer.at[pl.ds(2, 2)],
            dst_ref=buffer.at[pl.ds(0, 2)],
            send_sem=halo_send.at[phase, 1],
            recv_sem=halo_recv.at[phase, 1],
            device_id={"lat": lax.rem(me + 1, devices)},
            device_id_type=MESH,
        )
        return up, down

    def halo_start(buffer, phase):
        up, down = halo_copies(buffer, phase)

        @pl.when(me > 0)
        def _():
            up.start()

        @pl.when(me < devices - 1)
        def _():
            down.start()

    def halo_arrive(buffer, phase):
        up, down = halo_copies(buffer, phase)

        @pl.when(me < devices - 1)
        def _():
            up.wait_recv()

        @pl.when(me > 0)
        def _():
            down.wait_recv()

    def halo_sent(buffer, phase):
        up, down = halo_copies(buffer, phase)

        @pl.when(me > 0)
        def _():
            up.wait_send()

        @pl.when(me < devices - 1)
        def _():
            down.wait_send()

    def at(c, size=chunk):
        return pl.ds(pl.multiple_of(c * size, size), size)

    def around(c, shift):
        return pl.ds(pl.multiple_of(c * chunk + shift, 8), chunk + 8)

    def before(x):
        return pltpu.roll(x, 1, 0)[8:]

    def after(x):
        return pltpu.roll(x, chunk + 7, 0)[:chunk]

    def tall(x):
        return x.reshape(groups, 8, chans)

    sc = scale[...]
    for copy in fields:
        copy.wait()
    for j in range(span):

        def noisy(c, z):
            pad[2 + j, at(c)] = (
                state[j, at(c)].astype(F32) + sc * noise[j, at(c)].astype(F32)
            ).astype(BF16)
            return z

        lax.fori_loop(0, lons // chunk, noisy, 0)
        send[0, :, j] = (
            dot(fwd[...], pad[2 + j]).astype(BF16).reshape(devices, SLOTS, chans)
        )

    pl.semaphore_wait(barrier, devices - 1)
    exchange(0)
    halo_start(pad, 0)

    @pl.when(me == 0)
    def _():
        pad[0:2] = jnp.zeros((2, lons, chans), BF16)
        gpad[0:2] = jnp.zeros((2, lons, chans), BF16)

    @pl.when(me == devices - 1)
    def _():
        pad[4:6] = jnp.zeros((2, lons, chans), BF16)
        gpad[4:6] = jnp.zeros((2, lons, chans), BF16)

    def filter_row(row, t, s):
        total = jnp.zeros((1, chans), F32)
        for k in range(3):
            total = total + filt[((k * lats + row) * 3 + t) * 3 + s] * weight[k : k + 1, :]
        return total

    for i in range(span):
        for t in range(3):
            for s in range(3):
                cf[i * 9 + t * 3 + s] = jnp.broadcast_to(
                    filter_row(first + i, t, s), (8, chans)
                )
    for q in range(span):
        for e in range(5):
            row = lax.rem(first - 2 + q + e + lats, lats)
            taps = (2,) if e < 2 else ((0,) if e > 2 else (0, 1, 2))
            for s in range(3):
                total = jnp.zeros((1, chans), F32)
                for t in taps:
                    hit = jnp.where(rows[row * 3 + t] == first + q, 1.0, 0.0).astype(F32)
                    total = total + hit * filter_row(row, t, s)
                ef[q * 15 + e * 3 + s] = jnp.broadcast_to(total, (8, chans))

    arrive(0)

    def gather_rows(phase):
        block = recv[phase].reshape(devices * span * SLOTS, chans)
        pieces = max(devices // 16, 1)
        size = 2 * each * lats // pieces
        for piece in range(pieces):
            part = pl.ds(piece * size, size)
            pencil[part] = dot(pick[part], block).astype(BF16)

    def scatter_rows(phase):
        pieces = max(devices // 16, 1)
        size = devices // pieces
        for piece in range(pieces):
            part = pl.ds(piece * size * span * SLOTS, size * span * SLOTS)
            send[phase, pl.ds(piece * size, size)] = (
                dot(pick_t[part], sorted_rows[...]).astype(BF16).reshape(size, span, SLOTS, chans)
            )

    gather_rows(0)
    gains = gain[...]

    def analyse(m, z):
        for r in range(2):
            cm = dot(table[0, at(m, degrees)], pencil[at(2 * m + r, lats)])
            coef[2 * m + r] = cm
            sorted_rows[at(2 * m + r, lats)] = dot_turned(
                table[1, at(m, degrees)], (gains * cm).astype(BF16)
            ).astype(BF16)
        return z

    lax.fori_loop(0, each, analyse, 0)
    scatter_rows(1)
    exchange(1)

    halo_arrive(pad, 0)

    def picked(i, t, c):
        slot = jnp.clip(rows[(first + i) * 3 + t] - first + 2, 0, 5)
        return pad[slot, at(c)].astype(F32)

    for i in range(span):

        def taps_of(c, z):
            y = [None, None, None]
            for t in range(3):
                x = tall(picked(i, t, c))
                for s in range(3):
                    term = cf[i * 9 + t * 3 + s][None] * x
                    y[s] = term if t == 0 else y[s] + term
            here = pl.ds(pl.multiple_of(8 + c * chunk, 8), chunk)
            ysc[0, here] = y[0].reshape(chunk, chans)
            ysc[1, here] = y[2].reshape(chunk, chans)
            ls[i, at(c)] = y[1].reshape(chunk, chans)
            return z

        lax.fori_loop(0, lons // chunk, taps_of, 0)
        ysc[0, 7:8] = ysc[0, lons + 7 : lons + 8]
        ysc[1, lons + 8 : lons + 9] = ysc[1, 8:9]

        def join(c, z):
            ls[i, at(c)] += (
                before(ysc[0, around(c, 0)]) + after(ysc[1, around(c, 8)])
            )
            return z

        lax.fori_loop(0, lons // chunk, join, 0)

    arrive(1)

    root = math.sqrt(2.0 / math.pi)
    for j in range(span):
        returned = recv[1, :, j].reshape(devices * SLOTS, chans)

        def activate(c, z):
            v = ls[j, at(c, wide)] + dot(inv_t[at(c, wide)], returned)
            square = v * v
            th = jnp.tanh(root * v * (1.0 + 0.044715 * square))
            slope = 0.5 * (1.0 + th) + 0.5 * v * (1.0 - th * th) * root * (
                1.0 + 3 * 0.044715 * square
            )
            gpad[2 + j, at(c, wide)] = (cot[j, at(c, wide)].astype(F32) * slope).astype(BF16)
            return z

        lax.fori_loop(0, lons // wide, activate, 0)
        send[2, :, j] = (
            dot(inv[...], gpad[2 + j]).astype(BF16).reshape(devices, SLOTS, chans)
        )
    exchange(2)
    halo_start(gpad, 1)

    basis = [jnp.zeros((1, chans), F32) for _ in range(3)]
    for i in range(span):

        def widen(c, z):
            ysc[0, pl.ds(pl.multiple_of(8 + c * chunk, 8), chunk)] = gpad[2 + i, at(c)].astype(F32)
            return z

        lax.fori_loop(0, lons // chunk, widen, 0)
        ysc[0, 7:8] = ysc[0, lons + 7 : lons + 8]
        ysc[0, lons + 8 : lons + 9] = ysc[0, 8:9]

        def correlate(c, sums):
            g = [
                tall(after(ysc[0, around(c, 8)])),
                tall(ysc[0, pl.ds(pl.multiple_of(8 + c * chunk, 8), chunk)]),
                tall(before(ysc[0, around(c, 0)])),
            ]
            new = []
            for t in range(3):
                x = tall(picked(i, t, c))
                for s in range(3):
                    new.append(sums[t * 3 + s] + jnp.sum(g[s] * x, axis=0))
            return tuple(new)

        sums = lax.fori_loop(
            0, lons // chunk, correlate, tuple(jnp.zeros((8, chans), F32) for _ in range(9))
        )
        for t in range(3):
            for s in range(3):
                total = jnp.sum(sums[t * 3 + s], axis=0, keepdims=True)
                for k in range(3):
                    basis[k] = (
                        basis[k] + filt[((k * lats + first + i) * 3 + t) * 3 + s] * total
                    )
    small[...] = jnp.zeros((8, chans), F32)
    for k in range(3):
        small[k : k + 1] = basis[k]

    arrive(2)
    gather_rows(2)
    gacc[...] = jnp.zeros((degrees, chans), F32)

    def analyse_back(m, z):
        for r in range(2):
            gm = dot(table[1, at(m, degrees)], pencil[at(2 * m + r, lats)])
            gacc[...] += coef[2 * m + r] * gm
            sorted_rows[at(2 * m + r, lats)] = dot_turned(
                table[0, at(m, degrees)], (gains * gm).astype(BF16)
            ).astype(BF16)
        return z

    lax.fori_loop(0, each, analyse_back, 0)
    scatter_rows(3)
    exchange(3)

    def gain_copy(off, peer):
        return pltpu.make_async_remote_copy(
            src_ref=gacc.at[pl.ds(pl.multiple_of(lax.rem(peer, reducers) * 8, 8), 8)],
            dst_ref=gain_in.at[me],
            send_sem=gain_send.at[off],
            recv_sem=gain_recv.at[off],
            device_id={"lat": peer},
            device_id_type=MESH,
        )

    def total_copy(off, peer):
        return pltpu.make_async_remote_copy(
            src_ref=gain_sum.at[me],
            dst_ref=gain_sum.at[me],
            send_sem=gat_send.at[off],
            recv_sem=gat_recv.at[off],
            device_id={"lat": peer},
            device_id_type=MESH,
        )

    def gain_go(off, z):
        peer = peer_of(off)

        @pl.when(peer < reducers)
        def _():
            gain_copy(off, peer).start()

        return z

    lax.fori_loop(1, devices, gain_go, 0)

    halo_arrive(gpad, 1)
    for q in range(span):

        def spread_of(c, z):
            y = [None, None, None]
            for e in range(5):
                x = tall(gpad[q + e, at(c)].astype(F32))
                for s in range(3):
                    term = ef[q * 15 + e * 3 + s][None] * x
                    y[s] = term if e == 0 else y[s] + term
            here = pl.ds(pl.multiple_of(8 + c * chunk, 8), chunk)
            ysc[0, here] = y[2].reshape(chunk, chans)
            ysc[1, here] = y[0].reshape(chunk, chans)
            ls[q, at(c)] = y[1].reshape(chunk, chans)
            return z

        lax.fori_loop(0, lons // chunk, spread_of, 0)
        ysc[0, 7:8] = ysc[0, lons + 7 : lons + 8]
        ysc[1, lons + 8 : lons + 9] = ysc[1, 8:9]

        def join_back(c, z):
            ls[q, at(c)] += (
                before(ysc[0, around(c, 0)]) + after(ysc[1, around(c, 8)])
            )
            return z

        lax.fori_loop(0, lons // chunk, join_back, 0)

    @pl.when(me < reducers)
    def _():
        gain_in[me] = gacc[pl.ds(pl.multiple_of(lax.rem(me, reducers) * 8, 8), 8)]

        def take(off, z):
            gain_copy(off, peer_of(off)).wait_recv()
            return z

        lax.fori_loop(1, devices, take, 0)
        gain_sum[me] = jnp.sum(gain_in[...], axis=0)

        def give(off, z):
            total_copy(off, peer_of(off)).start()
            return z

        lax.fori_loop(1, devices, give, 0)

    arrive(3)
    accs = jnp.zeros((8, chans), F32)
    for j in range(span):
        back = recv[3, :, j].reshape(devices * SLOTS, chans)

        def finish(c, acc):
            total = ls[j, at(c, wide)] + dot(fwd_t[at(c, wide)], back)
            out[j, at(c, wide)] = total.astype(BF16)
            prod = total * noise[j, at(c, wide)].astype(F32)
            return acc + jnp.sum(prod.reshape(wide // 8, 8, chans), axis=0)

        accs = lax.fori_loop(0, lons // wide, finish, accs)
    small[3:4] = jnp.sum(accs, axis=0, keepdims=True)

    def small_copy(off, peer):
        return pltpu.make_async_remote_copy(
            src_ref=small,
            dst_ref=small_in.at[me],
            send_sem=small_send.at[off],
            recv_sem=small_recv.at[off],
            device_id={"lat": peer},
            device_id_type=MESH,
        )

    def small_go(off, z):
        small_copy(off, peer_of(off)).start()
        return z

    lax.fori_loop(1, devices, small_go, 0)
    small_in[me] = small[...]

    def gain_take(off, z):
        @pl.when(source_of(off) < reducers)
        def _():
            total_copy(off, peer_of(off)).wait_recv()

        return z

    lax.fori_loop(1, devices, gain_take, 0)
    gain_out[...] = gain_sum[0:reducers].reshape(degrees, chans)

    def small_take(off, z):
        small_copy(off, peer_of(off)).wait_recv()
        return z

    lax.fori_loop(1, devices, small_take, 0)
    sums = jnp.sum(small_in[...], axis=0)
    basis_out[...] = sums[0:3]
    scale_out[...] = sums[3:4]

    def sent(off, z):
        peer = peer_of(off)
        for phase in range(4):
            block_copy(phase, off, peer).wait_send()
        small_copy(off, peer).wait_send()

        @pl.when(peer < reducers)
        def _():
            gain_copy(off, peer).wait_send()

        @pl.when(me < reducers)
        def _():
            total_copy(off, peer).wait_send()

        return z

    lax.fori_loop(1, devices, sent, 0)
    halo_sent(pad, 0)
    halo_sent(gpad, 1)


def body(state, noise, scale, filt, rows, weight, gain, cot):
    devices = lax.axis_size("lat")
    span, lons, chans = state.shape
    degrees = gain.shape[0]
    lats = span * devices
    each = degrees // devices
    analysis, synthesis = legendre_numpy(degrees, lats, degrees)
    forward, inverse = fourier_numpy(lons, devices, each)

    tables = np.stack(
        [t.reshape(devices, each * degrees, lats) for t in (analysis, synthesis)], axis=1
    )
    table = lax.dynamic_index_in_dim(tables, lax.axis_index("lat"), 0, keepdims=False)
    pick = np.zeros((2 * each, lats, lats, SLOTS), jnp.bfloat16)
    for slot in range(2 * each):
        pick[slot, np.arange(lats), np.arange(lats), slot] = 1
    pick = pick.reshape(2 * each * lats, lats * SLOTS)
    vmem = pl.BlockSpec(memory_space=pltpu.VMEM)
    smem = pl.BlockSpec(memory_space=pltpu.SMEM)
    far = pl.BlockSpec(memory_space=pl.ANY)
    dma = pltpu.SemaphoreType.DMA
    out, basis, gains, scales = pl.pallas_call(
        functools.partial(kernel, (devices, each, lons, chans, degrees, lats)),
        out_shape=(
            jax.ShapeDtypeStruct((span, lons, chans), BF16),
            jax.ShapeDtypeStruct((3, chans), F32),
            jax.ShapeDtypeStruct((degrees, chans), F32),
            jax.ShapeDtypeStruct((1, chans), F32),
        ),
        in_specs=[smem, smem] + [far] * 3 + [vmem] * 10,
        out_specs=(vmem,) * 4,
        scratch_shapes=[
            pltpu.VMEM(state.shape, BF16),
            pltpu.VMEM(noise.shape, BF16),
            pltpu.VMEM(cot.shape, BF16),
            dma((3,)),
            pltpu.VMEM((6, lons, chans), BF16),
            pltpu.VMEM((6, lons, chans), BF16),
            pltpu.VMEM((2, lons, chans), F32),
            pltpu.VMEM((2, lons + 16, chans), F32),
            pltpu.VMEM((18, 8, chans), F32),
            pltpu.VMEM((30, 8, chans), F32),
            pltpu.VMEM((2 * each, degrees, chans), F32),
            pltpu.VMEM((degrees, chans), F32),
            pltpu.VMEM((2 * each * lats, chans), BF16),
            pltpu.VMEM((2 * each * lats, chans), BF16),
            pltpu.VMEM((4, devices, span, SLOTS, chans), BF16),
            pltpu.VMEM((4, devices, span, SLOTS, chans), BF16),
            pltpu.VMEM((devices, 8, chans), F32),
            pltpu.VMEM((devices, 8, chans), F32),
            pltpu.VMEM((8, chans), F32),
            pltpu.VMEM((devices, 8, chans), F32),
            dma((4, devices)),
            dma((4, devices)),
            dma((2, 2)),
            dma((2, 2)),
            dma((devices,)),
            dma((devices,)),
            dma((devices,)),
            dma((devices,)),
            dma((devices,)),
            dma((devices,)),
        ],
        compiler_params=pltpu.CompilerParams(
            collective_id=0, has_side_effects=True, vmem_limit_bytes=60 * 1024 * 1024
        ),
        name="block_and_gradient",
    )(
        filt.reshape(-1),
        rows.reshape(-1),
        state,
        noise,
        cot,
        scale.reshape(1, chans),
        weight,
        gain,
        forward,
        np.ascontiguousarray(forward.T),
        inverse,
        np.ascontiguousarray(inverse.T),
        pick,
        np.ascontiguousarray(pick.T),
        table,
    )
    return out, basis, gains, scales.reshape(chans)


def solution(mesh):
    field = P(("ens", "lat"), None, None)
    return jax.shard_map(
        body,
        mesh=mesh,
        in_specs=(field, field, P(), P(), P(), P(), P(), field),
        out_specs=(field, P("ens", None), P("ens", None), P("ens")),
        check_vma=False,
    )
```

```python
import functools
import math

import jax
import jax.numpy as jnp
import numpy as np
from jax import lax
from jax.experimental import pallas as pl
from jax.experimental.pallas import tpu as pltpu
from jax.sharding import PartitionSpec as P

F32, BF16 = jnp.float32, jnp.bfloat16
MESH = pl.DeviceIdType.MESH
SLOTS = 16


def legendre_numpy(modes, lats, degrees):
    u = np.pi * (np.arange(lats) + 0.5) / lats
    order = np.arange(modes, dtype=np.float64)[:, None]
    k = np.arange(1, modes + 1, dtype=np.float64)
    steps = np.concatenate([[0.0], np.cumsum(0.5 * np.log((2 * k + 1) / (2 * k)))])[:modes]
    start = np.exp(
        0.5 * np.log(1 / (4 * np.pi)) + steps[:, None] + order * np.log(np.sin(u))[None, :]
    )
    out = np.zeros((modes, degrees, lats))
    one = np.zeros((modes, lats))
    two = np.zeros((modes, lats))
    for l in range(degrees):
        a = np.sqrt((4.0 * l * l - 1 if l else 0.0) / np.maximum(l * l - order**2, 1.0))
        b = np.sqrt(
            np.maximum((l - 1.0) ** 2 - order**2, 0.0) / np.maximum(4 * (l - 1.0) ** 2 - 1, 1.0)
        )
        general = a * (np.cos(u)[None, :] * one - b * two)
        now = np.where(l < order, 0.0, np.where(l == order, start, general))
        out[:, l] = now
        one, two = now, one
    weight = np.pi / lats * np.sin(u)
    return (out * weight).astype(jnp.bfloat16), out.astype(jnp.bfloat16)


def fourier_numpy(lons, devices, each):
    modes = devices * each
    n = np.arange(lons)
    m = np.arange(modes)
    p = 2 * np.pi * ((n[None, :] * m[:, None]) % lons) / lons
    pair = np.stack([np.cos(p), -np.sin(p)], axis=1)
    forward = pair * (2 * np.pi / lons)
    inverse = pair * np.where(m == 0, 1.0, 2.0)[:, None, None]

    def padded(table):
        out = np.zeros((devices, SLOTS, lons))
        out[:, : 2 * each] = table.reshape(devices, 2 * each, lons)
        return out.reshape(devices * SLOTS, lons).astype(jnp.bfloat16)

    return padded(forward), padded(inverse)


def dot(a, b):
    return lax.dot_general(a, b, (((1,), (0,)), ((), ())), preferred_element_type=F32)


def dot_turned(a, b):
    return lax.dot_general(a, b, (((0,), (0,)), ((), ())), preferred_element_type=F32)


def kernel(
    dims,
    filt,
    rows,
    state_far,
    noise_far,
    cot_far,
    scale,
    weight,
    gain,
    fwd,
    fwd_t,
    inv,
    inv_t,
    pick,
    pick_t,
    table,
    out,
    basis_out,
    gain_out,
    scale_out,
    state,
    noise,
    cot,
    field_sem,
    pad,
    gpad,
    ls,
    ysc,
    cf,
    ef,
    coef,
    gacc,
    pencil,
    sorted_rows,
    send,
    recv,
    gain_in,
    gain_sum,
    small,
    small_in,
    a2a_send,
    a2a_recv,
    halo_send,
    halo_recv,
    gain_send,
    gain_recv,
    gat_send,
    gat_recv,
    small_send,
    small_recv,
):
    devices, each, lons, chans, degrees, lats = dims
    span = 2
    me = lax.axis_index("lat")
    first = me * span
    chunk, wide = 32, 128
    groups = chunk // 8
    reducers = degrees // 8

    def peer_of(off):
        return lax.rem(me + off, devices)

    def source_of(off):
        return lax.rem(me - off + devices, devices)

    fields = [
        pltpu.make_async_copy(src, dst, field_sem.at[i])
        for i, (src, dst) in enumerate(((state_far, state), (noise_far, noise), (cot_far, cot)))
    ]
    for copy in fields:
        copy.start()

    barrier = pltpu.get_barrier_semaphore()

    def greet(off, z):
        pl.semaphore_signal(barrier, inc=1, device_id={"lat": peer_of(off)}, device_id_type=MESH)
        return z

    lax.fori_loop(1, devices, greet, 0)

    def block_copy(phase, off, peer):
        return pltpu.make_async_remote_copy(
            src_ref=send.at[phase, peer],
            dst_ref=recv.at[phase, me],
            send_sem=a2a_send.at[phase, off],
            recv_sem=a2a_recv.at[phase, off],
            device_id={"lat": peer},
            device_id_type=MESH,
        )

    def exchange(phase):
        def go(off, z):
            block_copy(phase, off, peer_of(off)).start()
            return z

        lax.fori_loop(1, devices, go, 0)
        recv[phase, me] = send[phase, me]

    def arrive(phase):
        def take(off, z):
            block_copy(phase, off, peer_of(off)).wait_recv()
            return z

        lax.fori_loop(1, devices, take, 0)

    def halo_copies(buffer, phase):
        up = pltpu.make_async_remote_copy(
            src_ref=buffer.at[pl.ds(2, 2)],
            dst_ref=buffer.at[pl.ds(4, 2)],
            send_sem=halo_send.at[phase, 0],
            recv_sem=halo_recv.at[phase, 0],
            device_id={"lat": lax.rem(me + devices - 1, devices)},
            device_id_type=MESH,
        )
        down = pltpu.make_async_remote_copy(
            src_ref=buffer.at[pl.ds(2, 2)],
            dst_ref=buffer.at[pl.ds(0, 2)],
            send_sem=halo_send.at[phase, 1],
            recv_sem=halo_recv.at[phase, 1],
            device_id={"lat": lax.rem(me + 1, devices)},
            device_id_type=MESH,
        )
        return up, down

    def halo_start(buffer, phase):
        up, down = halo_copies(buffer, phase)

        @pl.when(me > 0)
        def _():
            up.start()

        @pl.when(me < devices - 1)
        def _():
            down.start()

    def halo_arrive(buffer, phase):
        up, down = halo_copies(buffer, phase)

        @pl.when(me < devices - 1)
        def _():
            up.wait_recv()

        @pl.when(me > 0)
        def _():
            down.wait_recv()

    def halo_sent(buffer, phase):
        up, down = halo_copies(buffer, phase)

        @pl.when(me > 0)
        def _():
            up.wait_send()

        @pl.when(me < devices - 1)
        def _():
            down.wait_send()

    def at(c, size=chunk):
        return pl.ds(pl.multiple_of(c * size, size), size)

    def around(c, shift):
        return pl.ds(pl.multiple_of(c * chunk + shift, 8), chunk + 8)

    def before(x):
        return pltpu.roll(x, 1, 0)[8:]

    def after(x):
        return pltpu.roll(x, chunk + 7, 0)[:chunk]

    def tall(x):
        return x.reshape(groups, 8, chans)

    sc = scale[...]
    for copy in fields:
        copy.wait()
    for j in range(span):

        def noisy(c, z):
            pad[2 + j, at(c)] = (
                state[j, at(c)].astype(F32) + sc * noise[j, at(c)].astype(F32)
            ).astype(BF16)
            return z

        lax.fori_loop(0, lons // chunk, noisy, 0, unroll=4)
        send[0, :, j] = (
            dot(fwd[...], pad[2 + j]).astype(BF16).reshape(devices, SLOTS, chans)
        )

    pl.semaphore_wait(barrier, devices - 1)
    exchange(0)
    halo_start(pad, 0)

    @pl.when(me == 0)
    def _():
        pad[0:2] = jnp.zeros((2, lons, chans), BF16)
        gpad[0:2] = jnp.zeros((2, lons, chans), BF16)

    @pl.when(me == devices - 1)
    def _():
        pad[4:6] = jnp.zeros((2, lons, chans), BF16)
        gpad[4:6] = jnp.zeros((2, lons, chans), BF16)

    def filter_row(row, t, s):
        total = jnp.zeros((1, chans), F32)
        for k in range(3):
            total = total + filt[((k * lats + row) * 3 + t) * 3 + s] * weight[k : k + 1, :]
        return total

    for i in range(span):
        for t in range(3):
            for s in range(3):
                cf[i * 9 + t * 3 + s] = jnp.broadcast_to(
                    filter_row(first + i, t, s), (8, chans)
                )
    for q in range(span):
        for e in range(5):
            row = lax.rem(first - 2 + q + e + lats, lats)
            taps = (2,) if e < 2 else ((0,) if e > 2 else (0, 1, 2))
            for s in range(3):
                total = jnp.zeros((1, chans), F32)
                for t in taps:
                    hit = jnp.where(rows[row * 3 + t] == first + q, 1.0, 0.0).astype(F32)
                    total = total + hit * filter_row(row, t, s)
                ef[q * 15 + e * 3 + s] = jnp.broadcast_to(total, (8, chans))

    arrive(0)

    def gather_rows(phase):
        block = recv[phase].reshape(devices * span * SLOTS, chans)
        pieces = max(devices // 16, 1)
        size = 2 * each * lats // pieces
        for piece in range(pieces):
            part = pl.ds(piece * size, size)
            pencil[part] = dot(pick[part], block).astype(BF16)

    def scatter_rows(phase):
        pieces = max(devices // 16, 1)
        size = devices // pieces
        for piece in range(pieces):
            part = pl.ds(piece * size * span * SLOTS, size * span * SLOTS)
            send[phase, pl.ds(piece * size, size)] = (
                dot(pick_t[part], sorted_rows[...]).astype(BF16).reshape(size, span, SLOTS, chans)
            )

    gather_rows(0)
    gains = gain[...]

    def analyse(m, z):
        for r in range(2):
            cm = dot(table[0, at(m, degrees)], pencil[at(2 * m + r, lats)])
            coef[2 * m + r] = cm
            sorted_rows[at(2 * m + r, lats)] = dot_turned(
                table[1, at(m, degrees)], (gains * cm).astype(BF16)
            ).astype(BF16)
        return z

    lax.fori_loop(0, each, analyse, 0)
    scatter_rows(1)
    exchange(1)

    halo_arrive(pad, 0)

    def picked(i, t, c):
        slot = jnp.clip(rows[(first + i) * 3 + t] - first + 2, 0, 5)
        return pad[slot, at(c)].astype(F32)

    for i in range(span):

        def taps_of(c, z):
            y = [None, None, None]
            for t in range(3):
                x = tall(picked(i, t, c))
                for s in range(3):
                    term = cf[i * 9 + t * 3 + s][None] * x
                    y[s] = term if t == 0 else y[s] + term
            here = pl.ds(pl.multiple_of(8 + c * chunk, 8), chunk)
            ysc[0, here] = y[0].reshape(chunk, chans)
            ysc[1, here] = y[2].reshape(chunk, chans)
            ls[i, at(c)] = y[1].reshape(chunk, chans)
            return z

        lax.fori_loop(0, lons // chunk, taps_of, 0, unroll=4)
        ysc[0, 7:8] = ysc[0, lons + 7 : lons + 8]
        ysc[1, lons + 8 : lons + 9] = ysc[1, 8:9]

        def join(c, z):
            ls[i, at(c)] += (
                before(ysc[0, around(c, 0)]) + after(ysc[1, around(c, 8)])
            )
            return z

        lax.fori_loop(0, lons // chunk, join, 0, unroll=4)

    arrive(1)

    root = math.sqrt(2.0 / math.pi)
    for j in range(span):
        returned = recv[1, :, j].reshape(devices * SLOTS, chans)

        def activate(c, z):
            v = ls[j, at(c, wide)] + dot(inv_t[at(c, wide)], returned)
            square = v * v
            th = jnp.tanh(root * v * (1.0 + 0.044715 * square))
            slope = 0.5 * (1.0 + th) + 0.5 * v * (1.0 - th * th) * root * (
                1.0 + 3 * 0.044715 * square
            )
            gpad[2 + j, at(c, wide)] = (cot[j, at(c, wide)].astype(F32) * slope).astype(BF16)
            return z

        lax.fori_loop(0, lons // wide, activate, 0)
        send[2, :, j] = (
            dot(inv[...], gpad[2 + j]).astype(BF16).reshape(devices, SLOTS, chans)
        )
    exchange(2)
    halo_start(gpad, 1)

    basis = [jnp.zeros((1, chans), F32) for _ in range(3)]
    for i in range(span):

        def widen(c, z):
            ysc[0, pl.ds(pl.multiple_of(8 + c * chunk, 8), chunk)] = gpad[2 + i, at(c)].astype(F32)
            return z

        lax.fori_loop(0, lons // chunk, widen, 0, unroll=4)
        ysc[0, 7:8] = ysc[0, lons + 7 : lons + 8]
        ysc[0, lons + 8 : lons + 9] = ysc[0, 8:9]

        def correlate(c, sums):
            g = [
                tall(after(ysc[0, around(c, 8)])),
                tall(ysc[0, pl.ds(pl.multiple_of(8 + c * chunk, 8), chunk)]),
                tall(before(ysc[0, around(c, 0)])),
            ]
            new = []
            for t in range(3):
                x = tall(picked(i, t, c))
                for s in range(3):
                    new.append(sums[t * 3 + s] + jnp.sum(g[s] * x, axis=0))
            return tuple(new)

        sums = lax.fori_loop(
            0, lons // chunk, correlate, tuple(jnp.zeros((8, chans), F32) for _ in range(9)), unroll=2
        )
        for t in range(3):
            for s in range(3):
                total = jnp.sum(sums[t * 3 + s], axis=0, keepdims=True)
                for k in range(3):
                    basis[k] = (
                        basis[k] + filt[((k * lats + first + i) * 3 + t) * 3 + s] * total
                    )
    small[...] = jnp.zeros((8, chans), F32)
    for k in range(3):
        small[k : k + 1] = basis[k]

    arrive(2)
    gather_rows(2)
    gacc[...] = jnp.zeros((degrees, chans), F32)

    def analyse_back(m, z):
        for r in range(2):
            gm = dot(table[1, at(m, degrees)], pencil[at(2 * m + r, lats)])
            gacc[...] += coef[2 * m + r] * gm
            sorted_rows[at(2 * m + r, lats)] = dot_turned(
                table[0, at(m, degrees)], (gains * gm).astype(BF16)
            ).astype(BF16)
        return z

    lax.fori_loop(0, each, analyse_back, 0)
    scatter_rows(3)
    exchange(3)

    def gain_copy(off, peer):
        return pltpu.make_async_remote_copy(
            src_ref=gacc.at[pl.ds(pl.multiple_of(lax.rem(peer, reducers) * 8, 8), 8)],
            dst_ref=gain_in.at[me],
            send_sem=gain_send.at[off],
            recv_sem=gain_recv.at[off],
            device_id={"lat": peer},
            device_id_type=MESH,
        )

    def total_copy(off, peer):
        return pltpu.make_async_remote_copy(
            src_ref=gain_sum.at[me],
            dst_ref=gain_sum.at[me],
            send_sem=gat_send.at[off],
            recv_sem=gat_recv.at[off],
            device_id={"lat": peer},
            device_id_type=MESH,
        )

    def gain_go(off, z):
        peer = peer_of(off)

        @pl.when(peer < reducers)
        def _():
            gain_copy(off, peer).start()

        return z

    lax.fori_loop(1, devices, gain_go, 0)

    halo_arrive(gpad, 1)
    for q in range(span):

        def spread_of(c, z):
            y = [None, None, None]
            for e in range(5):
                x = tall(gpad[q + e, at(c)].astype(F32))
                for s in range(3):
                    term = ef[q * 15 + e * 3 + s][None] * x
                    y[s] = term if e == 0 else y[s] + term
            here = pl.ds(pl.multiple_of(8 + c * chunk, 8), chunk)
            ysc[0, here] = y[2].reshape(chunk, chans)
            ysc[1, here] = y[0].reshape(chunk, chans)
            ls[q, at(c)] = y[1].reshape(chunk, chans)
            return z

        lax.fori_loop(0, lons // chunk, spread_of, 0, unroll=4)
        ysc[0, 7:8] = ysc[0, lons + 7 : lons + 8]
        ysc[1, lons + 8 : lons + 9] = ysc[1, 8:9]

        def join_back(c, z):
            ls[q, at(c)] += (
                before(ysc[0, around(c, 0)]) + after(ysc[1, around(c, 8)])
            )
            return z

        lax.fori_loop(0, lons // chunk, join_back, 0, unroll=4)

    @pl.when(me < reducers)
    def _():
        gain_in[me] = gacc[pl.ds(pl.multiple_of(lax.rem(me, reducers) * 8, 8), 8)]

        def take(off, z):
            gain_copy(off, peer_of(off)).wait_recv()
            return z

        lax.fori_loop(1, devices, take, 0)
        gain_sum[me] = jnp.sum(gain_in[...], axis=0)

        def give(off, z):
            total_copy(off, peer_of(off)).start()
            return z

        lax.fori_loop(1, devices, give, 0)

    arrive(3)
    accs = jnp.zeros((8, chans), F32)
    for j in range(span):
        back = recv[3, :, j].reshape(devices * SLOTS, chans)

        def finish(c, acc):
            total = ls[j, at(c, wide)] + dot(fwd_t[at(c, wide)], back)
            out[j, at(c, wide)] = total.astype(BF16)
            prod = total * noise[j, at(c, wide)].astype(F32)
            return acc + jnp.sum(prod.reshape(wide // 8, 8, chans), axis=0)

        accs = lax.fori_loop(0, lons // wide, finish, accs)
    small[3:4] = jnp.sum(accs, axis=0, keepdims=True)

    def small_copy(off, peer):
        return pltpu.make_async_remote_copy(
            src_ref=small,
            dst_ref=small_in.at[me],
            send_sem=small_send.at[off],
            recv_sem=small_recv.at[off],
            device_id={"lat": peer},
            device_id_type=MESH,
        )

    def small_go(off, z):
        small_copy(off, peer_of(off)).start()
        return z

    lax.fori_loop(1, devices, small_go, 0)
    small_in[me] = small[...]

    def gain_take(off, z):
        @pl.when(source_of(off) < reducers)
        def _():
            total_copy(off, peer_of(off)).wait_recv()

        return z

    lax.fori_loop(1, devices, gain_take, 0)
    gain_out[...] = gain_sum[0:reducers].reshape(degrees, chans)

    def small_take(off, z):
        small_copy(off, peer_of(off)).wait_recv()
        return z

    lax.fori_loop(1, devices, small_take, 0)
    sums = jnp.sum(small_in[...], axis=0)
    basis_out[...] = sums[0:3]
    scale_out[...] = sums[3:4]

    def sent(off, z):
        peer = peer_of(off)
        for phase in range(4):
            block_copy(phase, off, peer).wait_send()
        small_copy(off, peer).wait_send()

        @pl.when(peer < reducers)
        def _():
            gain_copy(off, peer).wait_send()

        @pl.when(me < reducers)
        def _():
            total_copy(off, peer).wait_send()

        return z

    lax.fori_loop(1, devices, sent, 0)
    halo_sent(pad, 0)
    halo_sent(gpad, 1)


def body(state, noise, scale, filt, rows, weight, gain, cot):
    devices = lax.axis_size("lat")
    span, lons, chans = state.shape
    degrees = gain.shape[0]
    lats = span * devices
    each = degrees // devices
    analysis, synthesis = legendre_numpy(degrees, lats, degrees)
    forward, inverse = fourier_numpy(lons, devices, each)

    tables = np.stack(
        [t.reshape(devices, each * degrees, lats) for t in (analysis, synthesis)], axis=1
    )
    table = lax.dynamic_index_in_dim(tables, lax.axis_index("lat"), 0, keepdims=False)
    pick = np.zeros((2 * each, lats, lats, SLOTS), jnp.bfloat16)
    for slot in range(2 * each):
        pick[slot, np.arange(lats), np.arange(lats), slot] = 1
    pick = pick.reshape(2 * each * lats, lats * SLOTS)
    vmem = pl.BlockSpec(memory_space=pltpu.VMEM)
    smem = pl.BlockSpec(memory_space=pltpu.SMEM)
    far = pl.BlockSpec(memory_space=pl.ANY)
    dma = pltpu.SemaphoreType.DMA
    out, basis, gains, scales = pl.pallas_call(
        functools.partial(kernel, (devices, each, lons, chans, degrees, lats)),
        out_shape=(
            jax.ShapeDtypeStruct((span, lons, chans), BF16),
            jax.ShapeDtypeStruct((3, chans), F32),
            jax.ShapeDtypeStruct((degrees, chans), F32),
            jax.ShapeDtypeStruct((1, chans), F32),
        ),
        in_specs=[smem, smem] + [far] * 3 + [vmem] * 10,
        out_specs=(vmem,) * 4,
        scratch_shapes=[
            pltpu.VMEM(state.shape, BF16),
            pltpu.VMEM(noise.shape, BF16),
            pltpu.VMEM(cot.shape, BF16),
            dma((3,)),
            pltpu.VMEM((6, lons, chans), BF16),
            pltpu.VMEM((6, lons, chans), BF16),
            pltpu.VMEM((2, lons, chans), F32),
            pltpu.VMEM((2, lons + 16, chans), F32),
            pltpu.VMEM((18, 8, chans), F32),
            pltpu.VMEM((30, 8, chans), F32),
            pltpu.VMEM((2 * each, degrees, chans), F32),
            pltpu.VMEM((degrees, chans), F32),
            pltpu.VMEM((2 * each * lats, chans), BF16),
            pltpu.VMEM((2 * each * lats, chans), BF16),
            pltpu.VMEM((4, devices, span, SLOTS, chans), BF16),
            pltpu.VMEM((4, devices, span, SLOTS, chans), BF16),
            pltpu.VMEM((devices, 8, chans), F32),
            pltpu.VMEM((devices, 8, chans), F32),
            pltpu.VMEM((8, chans), F32),
            pltpu.VMEM((devices, 8, chans), F32),
            dma((4, devices)),
            dma((4, devices)),
            dma((2, 2)),
            dma((2, 2)),
            dma((devices,)),
            dma((devices,)),
            dma((devices,)),
            dma((devices,)),
            dma((devices,)),
            dma((devices,)),
        ],
        compiler_params=pltpu.CompilerParams(
            collective_id=0, has_side_effects=True, vmem_limit_bytes=60 * 1024 * 1024
        ),
        name="block_and_gradient",
    )(
        filt.reshape(-1),
        rows.reshape(-1),
        state,
        noise,
        cot,
        scale.reshape(1, chans),
        weight,
        gain,
        forward,
        np.ascontiguousarray(forward.T),
        inverse,
        np.ascontiguousarray(inverse.T),
        pick,
        np.ascontiguousarray(pick.T),
        table,
    )
    return out, basis, gains, scales.reshape(chans)


def solution(mesh):
    field = P(("ens", "lat"), None, None)
    return jax.shard_map(
        body,
        mesh=mesh,
        in_specs=(field, field, P(), P(), P(), P(), P(), field),
        out_specs=(field, P("ens", None), P("ens", None), P("ens")),
        check_vma=False,
    )
```
